768 devices in a mesh: group: 96 (over z, x, core), head: 8 (over y).
Axes of the slice: x: 4, y: 8, z: 12, core: 2. Of those that a mesh axis runs over, the one named last changes fastest.
Arguments:
- query: bfloat16 [49152, 1792], P('group', 'head'), may hold values from -6 to 6
- key_in: bfloat16 [49152, 1792], P('group', 'head'), may hold values from -6 to 6
- value: bfloat16 [49152, 1792], P('group', 'head'), may hold values from -6 to 6
- proj: bfloat16 [1792, 2240], P('head'), may hold values from -0.125 to 0.125
- cot: bfloat16 [2240, 49152], P('head', 'group'), may hold values from -6 to 6
- lengths: int32 [96], replicated, may hold values from 128 to 512, as said below
Outputs:
- mixed: bfloat16 [2240, 49152], P('head', 'group')
- query_gradient: bfloat16 [49152, 1792], P('group', 'head')
- key_gradient: bfloat16 [49152, 1792], P('group', 'head')
- value_gradient: bfloat16 [49152, 1792], P('group', 'head')
The draws below stay inside these ranges and needn't reach their ends.
Inputs may be any that keep to these rules, and one draw needn't show every extreme that they name: `lengths`: every entry is a multiple of 128, and some block holds exactly 512 live tokens in every draw.
All inputs are finite; a program needn't handle non-finite values.
Results may differ from the reference program's by a relative error of at most 0.0067.
Values may be sent and summed in bfloat16 or wider, within the bound.
No kernel may reach another device: no remote copies, remote signals or barrier semaphores. Data moves between devices by JAX's collectives and lax.ppermute only.
A program may use at most 32 MiB of HBM per device.

```python
import jax
import jax.numpy as jnp
from jax import lax

MODEL_DIM = 2240
HEAD_DIM = 112
HEADS = 16
GROUP_CAP = 512
GROUPS = 96
TOKENS = 49152


def draw_lengths(key, part):
    key = jax.random.fold_in(key, 11)
    first, second = jax.random.split(key)
    top = GROUP_CAP // 128
    blocks = jax.random.randint(first, (GROUPS,), 1, top + 1)
    where_full = jax.random.randint(second, (), 0, GROUPS)
    blocks = jnp.where(jnp.arange(GROUPS) == where_full, top, blocks)
    return (blocks * 128).astype(jnp.int32)


def levels(own_key, extent, cuts, least, high):
    loudness, own = 1.0, jax.random.fold_in(own_key, 6)
    for axis_at, parts in cuts:
        heights = jnp.exp(jax.random.uniform(jax.random.fold_in(own, axis_at), (parts,), jnp.float32, least / len(cuts), high / len(cuts)))
        loudness = loudness * jnp.repeat(heights, extent[axis_at] // parts).reshape([-1 if axis == axis_at else 1 for axis in range(len(extent))])
    return loudness


def centred(own_key, dims, deviation, limit, pieces=(), kind=jnp.bfloat16):
    drawn = jax.random.normal(own_key, dims, jnp.float32) * deviation
    if len(pieces) > 0:
        drawn = levels(own_key, dims, pieces, -0.22, 0.18) * drawn
    return jnp.clip(drawn, min=-limit, max=limit).astype(kind)


def setup_inputs(seed: int = 0) -> dict:
    keys = jax.random.split(jax.random.key(seed), 7)
    query = centred(keys[0], (TOKENS, HEADS * HEAD_DIM), 1.0, 6.0, ((0, 96), (1, 8)))
    key_in = centred(keys[1], (TOKENS, HEADS * HEAD_DIM), 1.0, 6.0, ((0, 96), (1, 8)))
    value = centred(keys[2], (TOKENS, HEADS * HEAD_DIM), 1.0, 6.0, ((0, 96), (1, 8)))
    proj = centred(keys[3], (HEADS * HEAD_DIM, MODEL_DIM), (HEADS * HEAD_DIM) ** -0.5, 0.125, ((0, 8),))
    cot = centred(keys[4], (MODEL_DIM, TOKENS), 1.0, 6.0, ((0, 8), (1, 96)))
    lengths = draw_lengths(jax.random.fold_in(keys[6], 71), 0)
    return dict(query=query, key_in=key_in, value=value, proj=proj, cot=cot, lengths=lengths)


def masks(length, capacity_limit):
    pos = jnp.arange(capacity_limit, dtype=jnp.int32)
    valid_tokens = pos < length
    pair = (pos[:, None] >= pos[None, :]) & valid_tokens[:, None] & valid_tokens[None, :]
    return valid_tokens, pair


def local_weights(feat_q, key_features, pair):
    scores = jnp.einsum('thd,shd->hts', feat_q.astype(jnp.float32), key_features.astype(jnp.float32))
    masked = jnp.where(pair[None], scores, 0.0)
    return masked, masked.astype(jnp.bfloat16)


def reference(query, key_in, value, proj, cot, lengths):
    capacity_limit = GROUP_CAP
    heads = HEADS
    shape = (GROUPS, capacity_limit, heads, HEAD_DIM)
    feat_q = jax.nn.relu(query).reshape(shape)
    key_features = jax.nn.relu(key_in).reshape(shape)
    values = value.reshape(shape)
    unactivated_query = query.reshape(shape)
    unactivated_key = key_in.reshape(shape)
    high = lax.Precision.HIGHEST

    def forward(carry, item):
        state, ksum = carry
        fq, key_feature_rows, vv, length = item
        valid_tokens, pair = masks(length, capacity_limit)
        valid_mask = valid_tokens[:, None, None]
        masked_key_rows = jnp.where(valid_mask, key_feature_rows, jnp.zeros_like(key_feature_rows)).astype(jnp.float32)
        state_loc = jnp.einsum('shd,she->hde', masked_key_rows, vv.astype(jnp.float32))
        ksum_loc = jnp.sum(masked_key_rows, axis=0)
        masked, weights = local_weights(fq, key_feature_rows, pair)
        query_f = fq.astype(jnp.float32)
        numerator = jnp.einsum('hts,shd->thd', weights.astype(jnp.float32), vv.astype(jnp.float32))
        numerator = numerator + jnp.einsum('thd,hde->the', query_f, state, precision=high)
        denominator = jnp.sum(masked, axis=2).T + jnp.einsum('thd,hd->th', query_f, ksum, precision=high) + 1.0
        attention_block = jnp.where(valid_mask, numerator / denominator[:, :, None], 0.0).astype(jnp.bfloat16)
        return (state + state_loc, ksum + ksum_loc), (attention_block, numerator, denominator, state, ksum)

    zero_state = jnp.zeros((heads, HEAD_DIM, HEAD_DIM), jnp.float32)
    zero_sum = jnp.zeros((heads, HEAD_DIM), jnp.float32)
    unused, saved = lax.scan(forward, (zero_state, zero_sum), (feat_q, key_features, values, lengths))
    attention_block, numerator, denominator, state_prev, ksum_prev = saved
    attn_flat = attention_block.reshape(TOKENS, heads * HEAD_DIM)
    proj_f = proj.astype(jnp.float32)
    mixed = jnp.dot(attn_flat.astype(jnp.float32), proj_f, preferred_element_type=jnp.float32).T.astype(jnp.bfloat16)
    grad_attn = jnp.dot(cot.T.astype(jnp.float32), proj_f.T, preferred_element_type=jnp.float32).astype(jnp.bfloat16)
    grad_attn = lax.optimization_barrier(grad_attn).astype(jnp.float32).reshape(shape)

    def backward(carry, item):
        adj, adj_sum = carry
        fq, key_feature_rows, vv, rectified_query, rectified_key, length, attention_gradient, nu, denominator_gradient, sp, kp = item
        valid_tokens, pair = masks(length, capacity_limit)
        valid_mask = valid_tokens[:, None, None]
        masked, weights = local_weights(fq, key_feature_rows, pair)
        query_f = fq.astype(jnp.float32)
        key_f = key_feature_rows.astype(jnp.float32)
        val_f = vv.astype(jnp.float32)
        numerator_gradient = jnp.where(valid_mask, attention_gradient / denominator_gradient[:, :, None], 0.0)
        d_den = jnp.where(valid_tokens[:, None], -jnp.sum(attention_gradient * nu, axis=2) / (denominator_gradient * denominator_gradient), 0.0)
        d_num_b = numerator_gradient.astype(jnp.bfloat16).astype(jnp.float32)
        adj_loc = jnp.einsum('thd,the->hde', query_f, d_num_b)
        adj_sum_loc = jnp.einsum('th,thd->hd', d_den, query_f, precision=high)
        d_scores = jnp.einsum('the,she->hts', d_num_b, val_f) + d_den.T[:, :, None]
        d_scores = jnp.where(pair[None], d_scores, 0.0).astype(jnp.bfloat16).astype(jnp.float32)
        query_feature_gradient = jnp.einsum('hts,shd->thd', d_scores, key_f)
        query_feature_gradient = query_feature_gradient + jnp.einsum('the,hde->thd', numerator_gradient, sp, precision=high) + d_den[:, :, None] * kp[None]
        key_feature_gradient = jnp.einsum('hts,thd->shd', d_scores, query_f)
        key_feature_gradient = key_feature_gradient + jnp.einsum('she,hde->shd', val_f, adj, precision=high) + adj_sum[None]
        value_gradient_local = jnp.einsum('hts,the->she', weights.astype(jnp.float32), d_num_b)
        value_gradient_local = value_gradient_local + jnp.einsum('shd,hde->she', key_f, adj, precision=high)
        query_gradient_rows = jnp.where(valid_mask & (rectified_query > 0), query_feature_gradient, 0.0).astype(jnp.bfloat16)
        key_gradient_rows = jnp.where(valid_mask & (rectified_key > 0), key_feature_gradient, 0.0).astype(jnp.bfloat16)
        value_gradient_rows = jnp.where(valid_mask, value_gradient_local, 0.0).astype(jnp.bfloat16)
        return (adj + adj_loc, adj_sum + adj_sum_loc), (query_gradient_rows, key_gradient_rows, value_gradient_rows)

    items = (feat_q, key_features, values, unactivated_query, unactivated_key, lengths, grad_attn, numerator, denominator, state_prev, ksum_prev)
    unused, grads = lax.scan(backward, (zero_state, zero_sum), items, reverse=True)
    flat = (TOKENS, heads * HEAD_DIM)
    return mixed, grads[0].reshape(flat), grads[1].reshape(flat), grads[2].reshape(flat)
```

```python
import jax
import jax.numpy as jnp
from jax import lax
from jax.sharding import Mesh
from jax.sharding import PartitionSpec as P

HEAD_DIM = 112
PLANE = ("x", "c")
ROWS = 32


def shifted(block, distance):
    count = lax.axis_size("z")
    route = [(i - distance, i) for i in range(count) if 0 <= i - distance < count]
    return lax.ppermute(block, "z", route)


def sums_beyond(packed, sign):
    mine = lax.all_to_all(packed, PLANE, 0, 0)
    inner = mine if sign > 0 else mine[::-1]
    before = [jnp.zeros_like(inner[0])]
    for i in range(inner.shape[0]):
        before.append(before[-1] + inner[i])
    total = before.pop()
    near = shifted(total, sign) + shifted(total, 2 * sign) + shifted(total, 3 * sign)
    window = total + near
    base = near + shifted(window, 4 * sign) + shifted(window, 8 * sign)
    back = jnp.stack(before if sign > 0 else before[::-1]) + base[None]
    return lax.all_to_all(back, PLANE, 0, 0)


def pack(square, vector):
    heads = square.shape[0]
    flat = square.reshape(heads * HEAD_DIM, HEAD_DIM)
    rest = 8 * ROWS - flat.shape[0] - heads
    return jnp.concatenate(
        [flat, vector, jnp.zeros((rest, HEAD_DIM), jnp.float32)], axis=0
    ).reshape(8, ROWS, HEAD_DIM)


def unpack(packed, heads):
    flat = packed.reshape(8 * ROWS, HEAD_DIM)
    n = heads * HEAD_DIM
    return flat[:n].reshape(heads, HEAD_DIM, HEAD_DIM), flat[n : n + heads]


def halves(x):
    top = x.astype(jnp.bfloat16)
    return top, (x - top.astype(jnp.float32)).astype(jnp.bfloat16)


def dot2(spec, left, right):
    top, low = halves(right)
    return jnp.einsum(spec, left, top, preferred_element_type=jnp.float32) + jnp.einsum(
        spec, left, low, preferred_element_type=jnp.float32
    )


def per_device(query, key_in, value, proj, cot, lengths):
    bf, f32 = jnp.bfloat16, jnp.float32
    cap, width = query.shape
    heads = width // HEAD_DIM
    cot_all = lax.all_gather(cot, "y", axis=0, tiled=True)
    live = lengths[lax.axis_index(("z", "x", "c"))]
    slots = jnp.arange(cap, dtype=jnp.int32)
    valid = slots < live
    pair = (slots[:, None] >= slots[None, :]) & valid[:, None] & valid[None, :]
    vmask = valid[:, None, None]
    q3 = query.reshape(cap, heads, HEAD_DIM)
    k3 = key_in.reshape(cap, heads, HEAD_DIM)
    fq = jax.nn.relu(q3)
    fk = jax.nn.relu(k3)
    v3 = value.reshape(cap, heads, HEAD_DIM)
    fk_live = jnp.where(vmask, fk, jnp.zeros_like(fk))
    state_loc = jnp.einsum("shd,she->hde", fk_live, v3, preferred_element_type=f32)
    ksum_loc = jnp.sum(fk_live.astype(f32), axis=0)
    state_prev, ksum_prev = unpack(sums_beyond(pack(state_loc, ksum_loc), 1), heads)

    scores = jnp.einsum("thd,shd->hts", fq, fk, preferred_element_type=f32)
    masked = jnp.where(pair[None], scores, 0.0)
    weights = masked.astype(bf)
    fqf = fq.astype(f32)
    numer = jnp.einsum("hts,shd->thd", weights, v3, preferred_element_type=f32)
    numer = numer + dot2("thd,hde->the", fq, state_prev)
    denom = jnp.sum(masked, axis=2).T + jnp.sum(fqf * ksum_prev[None], axis=2) + 1.0
    inv = 1.0 / denom
    attn = jnp.where(vmask, numer * inv[:, :, None], 0.0).astype(bf).reshape(cap, width)
    terms = lax.dot_general(proj, attn, (((0,), (1,)), ((), ())), preferred_element_type=f32).astype(bf)
    cot_all, terms = lax.optimization_barrier((cot_all, terms))
    mixed = lax.psum_scatter(terms, "y", scatter_dimension=0, tiled=True)

    grad = lax.dot_general(cot_all, proj, (((0,), (1,)), ((), ())), preferred_element_type=f32)
    grad = grad.astype(bf).astype(f32).reshape(cap, heads, HEAD_DIM)
    d_num = jnp.where(vmask, grad * inv[:, :, None], 0.0)
    d_den = jnp.where(valid[:, None], -jnp.sum(grad * numer, axis=2) * inv * inv, 0.0)
    d_num_b = d_num.astype(bf)
    adj_loc = jnp.einsum("thd,the->hde", fq, d_num_b, preferred_element_type=f32)
    adj_sum_loc = jnp.sum(d_den[:, :, None] * fqf, axis=0)
    adj_next, adj_sum_next = unpack(sums_beyond(pack(adj_loc, adj_sum_loc), -1), heads)

    d_scores = jnp.einsum("the,she->hts", d_num_b, v3, preferred_element_type=f32) + d_den.T[:, :, None]
    d_scores = jnp.where(pair[None], d_scores, 0.0).astype(bf)
    gq = jnp.einsum("hts,shd->thd", d_scores, fk, preferred_element_type=f32)
    gq = gq + dot2("the,hde->thd", d_num_b, state_prev) + d_den[:, :, None] * ksum_prev[None]
    gk = jnp.einsum("hts,thd->shd", d_scores, fq, preferred_element_type=f32)
    gk = gk + dot2("she,hde->shd", v3, adj_next) + adj_sum_next[None]
    gv = jnp.einsum("hts,the->she", weights, d_num_b, preferred_element_type=f32)
    gv = gv + dot2("shd,hde->she", fk, adj_next)
    out_q = jnp.where(vmask & (q3 > 0), gq, 0.0).astype(bf).reshape(cap, width)
    out_k = jnp.where(vmask & (k3 > 0), gk, 0.0).astype(bf).reshape(cap, width)
    out_v = jnp.where(vmask, gv, 0.0).astype(bf).reshape(cap, width)
    return mixed, out_q, out_k, out_v


def solution(mesh):
    group, head = mesh.devices.shape
    fine = Mesh(mesh.devices.reshape(group // 8, 4, 2, head), ("z", "x", "c", "y"))
    tokens = ("z", "x", "c")
    return jax.shard_map(
        per_device,
        mesh=fine,
        in_specs=(P(tokens, "y"), P(tokens, "y"), P(tokens, "y"), P("y", None), P("y", tokens), P()),
        out_specs=(P("y", tokens), P(tokens, "y"), P(tokens, "y"), P(tokens, "y")),
        check_vma=False,
    )
```

```python
import jax
import jax.numpy as jnp
from jax import lax
from jax.experimental import pallas as pl
from jax.experimental.pallas import tpu as pltpu
from jax.sharding import Mesh
from jax.sharding import PartitionSpec as P

HD = 112
PAD = 128
PLANE = ("x", "c")
BF, F32 = jnp.bfloat16, jnp.float32
VMEM = pl.BlockSpec(memory_space=pltpu.VMEM)
SMEM = pl.BlockSpec(memory_space=pltpu.SMEM)
ANY = pl.BlockSpec(memory_space=pltpu.HBM)


def shape(dims, dtype):
    return jax.ShapeDtypeStruct(dims, dtype)


def call(body, outs, specs, name, cost=1000000):
    return pl.pallas_call(
        body,
        out_shape=outs,
        in_specs=specs,
        out_specs=jax.tree.map(lambda _: VMEM, outs),
        compiler_params=pltpu.CompilerParams(vmem_limit_bytes=40 * 1024 * 1024),
        cost_estimate=pl.CostEstimate(flops=cost, bytes_accessed=cost, transcendentals=0),
        name=name,
    )


def nn(a, b):
    return lax.dot_general(a, b, (((1,), (0,)), ((), ())), preferred_element_type=F32)


def nt(a, b):
    return lax.dot_general(a, b, (((1,), (1,)), ((), ())), preferred_element_type=F32)


def halves(x):
    top = x.astype(BF)
    return top, (x - top.astype(F32)).astype(BF)


def relu(x):
    return jnp.maximum(x, jnp.zeros_like(x))


def with_ones(v):
    row = lax.broadcasted_iota(jnp.int32, (PAD - HD, v.shape[1]), 0)
    return jnp.concatenate([v, (row < 2).astype(F32).astype(BF)], axis=0)


def taller(x):
    return jnp.concatenate([x, jnp.zeros((PAD - HD, x.shape[1]), x.dtype)], axis=0)


def live_row(live, n):
    return lax.broadcasted_iota(jnp.int32, (1, n), 1) < live


def causal(rows, cols, row0):
    t = lax.broadcasted_iota(jnp.int32, (rows, cols), 0) + row0
    return t >= lax.broadcasted_iota(jnp.int32, (rows, cols), 1)


def rows_of(h):
    return slice(h * HD, (h + 1) * HD)


def state_kernel(live_ref, k_ref, v_ref, out_ref):
    n = k_ref.shape[1]
    ok = live_row(live_ref[0], n)
    for h in range(k_ref.shape[0] // HD):
        fk = jnp.where(ok, relu(k_ref[rows_of(h)]).astype(F32), 0.0).astype(BF)
        out_ref[h * PAD : (h + 1) * PAD] = nt(with_ones(v_ref[rows_of(h)]), taller(fk))


def total_kernel(mine_ref, out_ref):
    total = jnp.sum(mine_ref[...], axis=0).astype(BF)
    for i in range(out_ref.shape[0]):
        out_ref[i] = total


def spread_kernel(sign, z_ref, mine_ref, all_ref, out_ref):
    z = z_ref[0]
    base = jnp.zeros(mine_ref.shape[1:], F32)
    for i in range(all_ref.shape[0]):
        keep = (i < z) if sign > 0 else (i > z)
        base = base + jnp.where(keep, all_ref[i].astype(F32), 0.0)
    steps = range(mine_ref.shape[0])
    for i in steps if sign > 0 else reversed(steps):
        out_ref[i] = base
        base = base + mine_ref[i]


def sums_beyond(packed, z, sign):
    count = lax.axis_size("z")
    rows = packed.shape[0] // 8
    mine = lax.all_to_all(packed.reshape(8, rows, PAD), PLANE, 0, 0)
    totals = call(total_kernel, shape((count, rows, PAD), BF), [VMEM], "plane_total")(mine)
    everyone = lax.all_to_all(totals, "z", 0, 0)
    back = call(
        lambda *refs: spread_kernel(sign, *refs), shape((8, rows, PAD), F32), [SMEM, VMEM, VMEM], "spread"
    )(z, mine, everyone)
    return lax.all_to_all(back, PLANE, 0, 0).reshape(8 * rows, PAD)


def weights_kernel(q_ref, k_ref, v_ref, w_ref, num_ref):
    n = q_ref.shape[1]
    half = n // 2
    for h in range(q_ref.shape[0] // HD):
        fq = relu(q_ref[rows_of(h)])
        fk = relu(k_ref[rows_of(h)])
        va = with_ones(v_ref[rows_of(h)])
        fqt = taller(fq).astype(F32).T.astype(BF)
        fk = taller(fk)
        for i in range(2):
            cols = half * (i + 1)
            s = nn(fqt[i * half : (i + 1) * half], fk[:, :cols])
            w = jnp.where(causal(half, cols, i * half), s, 0.0).astype(BF)
            w_ref[h, i * half : (i + 1) * half, :cols] = w
            if i == 0:
                w_ref[h, :half, half:] = jnp.zeros((half, half), BF)
            num_ref[h * PAD : (h + 1) * PAD, i * half : (i + 1) * half] = nt(va[:, :cols], w)


def attend_kernel(live_ref, q_ref, num_ref, st_ref, attn_ref, numer_ref):
    n = q_ref.shape[1]
    ok = live_row(live_ref[0], n)
    for h in range(q_ref.shape[0] // HD):
        at = slice(h * PAD, (h + 1) * PAD)
        fq = taller(relu(q_ref[rows_of(h)]))
        top, low = halves(st_ref[at])
        numer = num_ref[at] + (nn(top, fq) + nn(low, fq))
        numer_ref[at] = numer
        inv = 1.0 / (numer[HD : HD + 1] + 1.0)
        attn_ref[rows_of(h)] = jnp.where(ok, numer[:HD] * inv, 0.0).astype(BF)


def adjoint_kernel(live_ref, cot_ref, proj_ref, q_ref, numer_ref, after_ref, dn_ref, adj_ref):
    n = q_ref.shape[1]
    ok = live_row(live_ref[0], n)
    grad = nn(proj_ref[...], cot_ref[...]).astype(BF).astype(F32)
    row = lax.broadcasted_iota(jnp.int32, (PAD - HD, n), 0)
    for h in range(q_ref.shape[0] // HD):
        at = slice(h * PAD, (h + 1) * PAD)
        numer = numer_ref[at]
        inv = 1.0 / (numer[HD : HD + 1] + 1.0)
        g = grad[rows_of(h)]
        dn = jnp.where(ok, g * inv, 0.0).astype(BF)
        dd = jnp.where(ok, -jnp.sum(g * numer[:HD], axis=0, keepdims=True) * inv * inv, 0.0)
        top = dd.astype(BF).astype(F32)
        tail = jnp.where(row == 0, top, jnp.where(row == 1, dd - top, 0.0)).astype(BF)
        dna = jnp.concatenate([dn, tail], axis=0)
        dn_ref[at] = dna
        adj_ref[at] = nt(taller(relu(q_ref[rows_of(h)])), dna)


def local_grad_kernel(live_ref, q_ref, k_ref, v_ref, w_ref, dn_ref, st_ref, gq_ref, gk_ref, gv_ref):
    n = q_ref.shape[1]
    half = n // 2
    ok = live_row(live_ref[0], n)
    for h in range(q_ref.shape[0] // HD):
        at = slice(h * PAD, (h + 1) * PAD)
        q = q_ref[rows_of(h)]
        fq = relu(q)
        fk = relu(k_ref[rows_of(h)])
        va = with_ones(v_ref[rows_of(h)])
        dna = dn_ref[at]
        dnt = dna.astype(F32).T.astype(BF)
        d0 = jnp.where(causal(half, half, 0), nn(dnt[:half], va[:, :half]), 0.0).astype(BF)
        d1 = jnp.where(causal(half, n, half), nn(dnt[half:], va), 0.0).astype(BF)
        st = st_ref[at].T
        top, low = halves(st)
        dd = dna[HD : HD + 1].astype(F32) + dna[HD + 1 : HD + 2].astype(F32)
        bare = jnp.concatenate([dna[:HD], jnp.zeros((PAD - HD, n), BF)], axis=0)
        gq = jnp.concatenate([nt(fk[:, :half], d0), nt(fk, d1)], axis=1)
        gq = gq + (nn(top, bare) + nn(low, bare))[:HD] + st[:HD, HD : HD + 1] * dd
        gq_ref[rows_of(h)] = jnp.where(ok & (q.astype(F32) > 0), gq, 0.0).astype(BF)
        gk = nn(fq[:, half:], d1)
        gk_ref[rows_of(h), half:] = gk[:, half:]
        gk_ref[rows_of(h), :half] = gk[:, :half] + nn(fq[:, :half], d0)
        gv_ref[rows_of(h)] = nn(dna[:HD], w_ref[h])


def far_grad_kernel(live_ref, k_ref, v_ref, gk_ref, gv_ref, adj_ref, outk_ref, outv_ref):
    n = k_ref.shape[1]
    ok = live_row(live_ref[0], n)
    for h in range(k_ref.shape[0] // HD):
        adj = adj_ref[h * PAD : (h + 1) * PAD]
        k = k_ref[rows_of(h)]
        fk = taller(relu(k))
        va = with_ones(v_ref[rows_of(h)])
        top, low = halves(adj)
        gk = gk_ref[rows_of(h)] + (nn(top, va) + nn(low, va))[:HD]
        outk_ref[rows_of(h)] = jnp.where(ok & (k.astype(F32) > 0), gk, 0.0).astype(BF)
        top, low = halves(adj.T)
        gv = gv_ref[rows_of(h)] + (nn(top, fk) + nn(low, fk))[:HD]
        outv_ref[rows_of(h)] = jnp.where(ok, gv, 0.0).astype(BF)


def per_device(query, key_in, value, proj, cot, lengths):
    q, k, v = query.T, key_in.T, value.T
    width, n = q.shape
    heads = width // HD
    live = lax.dynamic_slice(lengths, (lax.axis_index(("z", "x", "c")),), (1,))
    z = lax.axis_index("z").astype(jnp.int32).reshape(1)
    cot_all = lax.all_gather(cot, "y", axis=0, tiled=True)
    packed = call(state_kernel, shape((heads * PAD, PAD), F32), [SMEM, VMEM, VMEM], "own_state")(live, k, v)
    state = sums_beyond(packed, z, 1)
    w, num = call(
        weights_kernel,
        (shape((heads, n, n), BF), shape((heads * PAD, n), F32)),
        [VMEM] * 3,
        "own_weights",
    )(q, k, v)
    attn, numer = call(
        attend_kernel,
        (shape((width, n), BF), shape((heads * PAD, n), F32)),
        [SMEM] + [VMEM] * 3,
        "attend",
    )(live, q, num, state)
    terms = lax.dot_general(proj, attn, (((0,), (0,)), ((), ())), preferred_element_type=F32).astype(BF)
    mixed = lax.psum_scatter(terms, "y", scatter_dimension=0, tiled=True)
    dn, adj = call(
        adjoint_kernel,
        (shape((heads * PAD, n), BF), shape((heads * PAD, PAD), F32)),
        [SMEM] + [VMEM] * 4 + [ANY],
        "own_adjoint",
    )(live, cot_all, proj, q, numer, terms)
    adj_next = sums_beyond(adj, z, -1)
    gq, gk, gv = call(
        local_grad_kernel,
        (shape((width, n), BF), shape((width, n), F32), shape((width, n), F32)),
        [SMEM] + [VMEM] * 6,
        "own_gradients",
    )(live, q, k, v, w, dn, state)
    gk, gv = call(
        far_grad_kernel,
        (shape((width, n), BF), shape((width, n), BF)),
        [SMEM] + [VMEM] * 5,
        "far_gradients",
    )(live, k, v, gk, gv, adj_next)
    return mixed, gq.T, gk.T, gv.T


def solution(mesh):
    group, head = mesh.devices.shape
    fine = Mesh(mesh.devices.reshape(group // 8, 4, 2, head), ("z", "x", "c", "y"))
    tokens = ("z", "x", "c")
    return jax.shard_map(
        per_device,
        mesh=fine,
        in_specs=(P(tokens, "y"), P(tokens, "y"), P(tokens, "y"), P("y", None), P("y", tokens), P()),
        out_specs=(P("y", tokens), P(tokens, "y"), P(tokens, "y"), P(tokens, "y")),
        check_vma=False,
    )
```

```python
import jax
import jax.numpy as jnp
from jax import lax
from jax.experimental import pallas as pl
from jax.experimental.pallas import tpu as pltpu
from jax.sharding import Mesh
from jax.sharding import PartitionSpec as P

HD = 112
PAD = 128
PLANE = ("x", "c")
BF, F32 = jnp.bfloat16, jnp.float32
VMEM = pl.BlockSpec(memory_space=pltpu.VMEM)
SMEM = pl.BlockSpec(memory_space=pltpu.SMEM)
STEP = 640
LIMIT = 16 * 1024 * 1024


def shape(dims, dtype):
    return jax.ShapeDtypeStruct(dims, dtype)


def call(body, outs, specs, name, cost=1000000):
    return pl.pallas_call(
        body,
        out_shape=outs,
        in_specs=specs,
        out_specs=jax.tree.map(lambda _: VMEM, outs),
        compiler_params=pltpu.CompilerParams(vmem_limit_bytes=LIMIT),
        cost_estimate=pl.CostEstimate(flops=cost, bytes_accessed=cost, transcendentals=0),
        name=name,
    )


def nn(a, b):
    return lax.dot_general(a, b, (((1,), (0,)), ((), ())), preferred_element_type=F32)


def nt(a, b):
    return lax.dot_general(a, b, (((1,), (1,)), ((), ())), preferred_element_type=F32)


def halves(x):
    top = x.astype(BF)
    return top, (x - top.astype(F32)).astype(BF)


def relu(x):
    return jnp.maximum(x, jnp.zeros_like(x))


def with_ones(v):
    row = lax.broadcasted_iota(jnp.int32, (PAD - HD, v.shape[1]), 0)
    return jnp.concatenate([v, (row < 2).astype(F32).astype(BF)], axis=0)


def taller(x):
    return jnp.concatenate([x, jnp.zeros((PAD - HD, x.shape[1]), x.dtype)], axis=0)


def live_row(place_ref, lengths_ref, n):
    return lax.broadcasted_iota(jnp.int32, (1, n), 1) < lengths_ref[place_ref[0]]


def causal(rows, cols, row0):
    t = lax.broadcasted_iota(jnp.int32, (rows, cols), 0) + row0
    return t >= lax.broadcasted_iota(jnp.int32, (rows, cols), 1)


def rows_of(h):
    return slice(h * HD, (h + 1) * HD)


def state_kernel(place_ref, lengths_ref, k_ref, v_ref, out_ref):
    n = k_ref.shape[1]
    ok = live_row(place_ref, lengths_ref, n)
    for h in range(k_ref.shape[0] // HD):
        fk = jnp.where(ok, relu(k_ref[rows_of(h)]).astype(F32), 0.0).astype(BF)
        out_ref[h * PAD : (h + 1) * PAD] = nt(with_ones(v_ref[rows_of(h)]), taller(fk))


def total_kernel(mine_ref, after_ref, out_ref):
    total = jnp.sum(mine_ref[...], axis=0).astype(BF)
    for i in range(out_ref.shape[0]):
        out_ref[i] = total


def spread_kernel(sign, z_ref, mine_ref, all_ref, out_ref):
    z = z_ref[0]
    base = jnp.zeros(mine_ref.shape[1:], F32)
    for i in range(all_ref.shape[0]):
        keep = (i < z) if sign > 0 else (i > z)
        base = base + jnp.where(keep, all_ref[i].astype(F32), 0.0)
    steps = range(mine_ref.shape[0])
    for i in steps if sign > 0 else reversed(steps):
        out_ref[i] = base
        base = base + mine_ref[i]


def sums_beyond(packed, z, sign, after):
    count = lax.axis_size("z")
    rows = packed.shape[0] // 8
    mine = lax.all_to_all(packed.reshape(8, rows, PAD), PLANE, 0, 0)
    totals = call(total_kernel, shape((count, rows, PAD), BF), [VMEM] * 2, "plane_total")(mine, after)
    everyone = lax.all_to_all(totals, "z", 0, 0)
    back = call(
        lambda *refs: spread_kernel(sign, *refs), shape((8, rows, PAD), F32), [SMEM, VMEM, VMEM], "spread"
    )(z, mine, everyone)
    return lax.all_to_all(back, PLANE, 0, 0).reshape(8 * rows, PAD)


def weights_of(fq, fk, half, i):
    cols = half * (i + 1)
    fqt = taller(fq[:, i * half : (i + 1) * half]).astype(F32).T.astype(BF)
    s = nn(fqt, taller(fk)[:, :cols])
    return jnp.where(causal(half, cols, i * half), s, 0.0).astype(BF)


def weights_kernel(q_ref, k_ref, v_ref, num_ref, token_ref):
    token_ref[...] = jnp.zeros(token_ref.shape, F32)
    n = q_ref.shape[1]
    half = n // 2
    for h in range(q_ref.shape[0] // HD):
        fq = relu(q_ref[rows_of(h)])
        fk = relu(k_ref[rows_of(h)])
        va = with_ones(v_ref[rows_of(h)])
        for i in range(2):
            w = weights_of(fq, fk, half, i)
            num_ref[h * PAD : (h + 1) * PAD, i * half : (i + 1) * half] = nt(va[:, : half * (i + 1)], w)


def attend_kernel(
    place_ref, lengths_ref, q_ref, num_ref, st_ref, proj_ref, terms_ref, numer_ref, token_ref
):
    n = q_ref.shape[1]
    ok = live_row(place_ref, lengths_ref, n)
    attn = []
    for h in range(q_ref.shape[0] // HD):
        at = slice(h * PAD, (h + 1) * PAD)
        fq = taller(relu(q_ref[rows_of(h)]))
        top, low = halves(st_ref[at])
        numer = num_ref[at] + (nn(top, fq) + nn(low, fq))
        numer_ref[at] = numer
        inv = 1.0 / (numer[HD : HD + 1] + 1.0)
        attn.append(jnp.where(ok, numer[:HD] * inv, 0.0).astype(BF))
    attn = jnp.concatenate(attn, axis=0)
    features = proj_ref.shape[1]
    for start in range(0, features, STEP):
        part = slice(start, min(start + STEP, features))
        terms_ref[part] = nn(proj_ref[:, part].astype(F32).T.astype(BF), attn).astype(BF)
    token_ref[...] = jnp.zeros(token_ref.shape, F32)


def adjoint_kernel(place_ref, lengths_ref, cot_ref, proj_ref, q_ref, numer_ref, after_ref, dn_ref, adj_ref):
    n = q_ref.shape[1]
    ok = live_row(place_ref, lengths_ref, n)
    grad = nn(proj_ref[...], cot_ref[...]).astype(BF).astype(F32)
    row = lax.broadcasted_iota(jnp.int32, (PAD - HD, n), 0)
    for h in range(q_ref.shape[0] // HD):
        at = slice(h * PAD, (h + 1) * PAD)
        numer = numer_ref[at]
        inv = 1.0 / (numer[HD : HD + 1] + 1.0)
        g = grad[rows_of(h)]
        dn = jnp.where(ok, g * inv, 0.0).astype(BF)
        dd = jnp.where(ok, -jnp.sum(g * numer[:HD], axis=0, keepdims=True) * inv * inv, 0.0)
        top = dd.astype(BF).astype(F32)
        tail = jnp.where(row == 0, top, jnp.where(row == 1, dd - top, 0.0)).astype(BF)
        dna = jnp.concatenate([dn, tail], axis=0)
        dn_ref[at] = dna
        adj_ref[at] = nt(taller(relu(q_ref[rows_of(h)])), dna)


def local_grad_kernel(place_ref, lengths_ref, q_ref, k_ref, v_ref, dn_ref, st_ref, gq_ref, gk_ref, gv_ref, token_ref):
    token_ref[...] = jnp.zeros(token_ref.shape, F32)
    n = q_ref.shape[1]
    half = n // 2
    ok = live_row(place_ref, lengths_ref, n)
    for h in range(q_ref.shape[0] // HD):
        at = slice(h * PAD, (h + 1) * PAD)
        q = q_ref[rows_of(h)]
        fq = relu(q)
        fk = relu(k_ref[rows_of(h)])
        va = with_ones(v_ref[rows_of(h)])
        dna = dn_ref[at]
        dnt = dna.astype(F32).T.astype(BF)
        d0 = jnp.where(causal(half, half, 0), nn(dnt[:half], va[:, :half]), 0.0).astype(BF)
        d1 = jnp.where(causal(half, n, half), nn(dnt[half:], va), 0.0).astype(BF)
        st = st_ref[at].T
        top, low = halves(st)
        dd = dna[HD : HD + 1].astype(F32) + dna[HD + 1 : HD + 2].astype(F32)
        bare = jnp.concatenate([dna[:HD], jnp.zeros((PAD - HD, n), BF)], axis=0)
        gq = jnp.concatenate([nt(fk[:, :half], d0), nt(fk, d1)], axis=1)
        gq = gq + (nn(top, bare) + nn(low, bare))[:HD] + st[:HD, HD : HD + 1] * dd
        gq_ref[rows_of(h)] = jnp.where(ok & (q.astype(F32) > 0), gq, 0.0).astype(BF)
        gk = nn(fq[:, half:], d1)
        gk_ref[rows_of(h), half:] = gk[:, half:]
        gk_ref[rows_of(h), :half] = gk[:, :half] + nn(fq[:, :half], d0)
        gv = nn(dna[:HD, half:], weights_of(fq, fk, half, 1))
        gv_ref[rows_of(h), half:] = gv[:, half:]
        gv_ref[rows_of(h), :half] = gv[:, :half] + nn(dna[:HD, :half], weights_of(fq, fk, half, 0))


def far_grad_kernel(place_ref, lengths_ref, k_ref, v_ref, gk_ref, gv_ref, adj_ref, outk_ref, outv_ref):
    n = k_ref.shape[1]
    ok = live_row(place_ref, lengths_ref, n)
    for h in range(k_ref.shape[0] // HD):
        adj = adj_ref[h * PAD : (h + 1) * PAD]
        k = k_ref[rows_of(h)]
        fk = taller(relu(k))
        va = with_ones(v_ref[rows_of(h)])
        top, low = halves(adj)
        gk = gk_ref[rows_of(h)] + (nn(top, va) + nn(low, va))[:HD]
        outk_ref[rows_of(h)] = jnp.where(ok & (k.astype(F32) > 0), gk, 0.0).astype(BF)
        top, low = halves(adj.T)
        gv = gv_ref[rows_of(h)] + (nn(top, fk) + nn(low, fk))[:HD]
        outv_ref[rows_of(h)] = jnp.where(ok, gv, 0.0).astype(BF)


def per_device(query, key_in, value, proj, cot, lengths):
    q, k, v = query.T, key_in.T, value.T
    width, n = q.shape
    heads = width // HD
    place = lax.axis_index(("z", "x", "c")).astype(jnp.int32).reshape(1)
    token = shape((8, 128), F32)
    z = lax.axis_index("z").astype(jnp.int32).reshape(1)
    cot_all = lax.all_gather(cot, "y", axis=0, tiled=True)
    packed = call(state_kernel, shape((heads * PAD, PAD), F32), [SMEM] * 2 + [VMEM] * 2, "own_state")(place, lengths, k, v)
    num, weighed = call(weights_kernel, (shape((heads * PAD, n), F32), token), [VMEM] * 3, "own_weights")(q, k, v)
    state = sums_beyond(packed, z, 1, weighed)
    terms, numer, summed = call(
        attend_kernel,
        (shape((proj.shape[1], n), BF), shape((heads * PAD, n), F32), token),
        [SMEM] * 2 + [VMEM] * 4,
        "attend",
    )(place, lengths, q, num, state, proj)
    mixed = lax.psum_scatter(terms, "y", scatter_dimension=0, tiled=True)
    dn, adj = call(
        adjoint_kernel,
        (shape((heads * PAD, n), BF), shape((heads * PAD, PAD), F32)),
        [SMEM] * 2 + [VMEM] * 5,
        "own_adjoint",
    )(place, lengths, cot_all, proj, q, numer, summed)
    gq, gk, gv, gradients = call(
        local_grad_kernel,
        (shape((width, n), BF), shape((width, n), F32), shape((width, n), F32), token),
        [SMEM] * 2 + [VMEM] * 5,
        "own_gradients",
    )(place, lengths, q, k, v, dn, state)
    adj_next = sums_beyond(adj, z, -1, gradients)
    gk, gv = call(
        far_grad_kernel,
        (shape((width, n), BF), shape((width, n), BF)),
        [SMEM] * 2 + [VMEM] * 5,
        "far_gradients",
    )(place, lengths, k, v, gk, gv, adj_next)
    return mixed, gq.T, gk.T, gv.T


def solution(mesh):
    group, head = mesh.devices.shape
    fine = Mesh(mesh.devices.reshape(group // 8, 4, 2, head), ("z", "x", "c", "y"))
    tokens = ("z", "x", "c")
    return jax.shard_map(
        per_device,
        mesh=fine,
        in_specs=(P(tokens, "y"), P(tokens, "y"), P(tokens, "y"), P("y", None), P("y", tokens), P()),
        out_specs=(P("y", tokens), P(tokens, "y"), P(tokens, "y"), P(tokens, "y")),
        check_vma=False,
    )
```
